768 devices in a mesh: branch: 12 (over x, z_hi), shard: 64 (over z_lo, y, core).
Axes of the slice: x: 4, y: 8, z: 12 (z_hi: 3, z_lo: 4; z = z_hi * 4 + z_lo), core: 2. Of those that a mesh axis runs over, the one named last changes fastest.
Arguments:
- resid: bfloat16 [2304, 4096], P('branch', 'shard'), may hold values from -6 to 6
- context: bfloat16 [2304, 4096], P('branch'), may hold values from -6 to 6
- o_weight: bfloat16 [12, 4096, 4096], P('branch', None, 'shard'), may hold values from -0.3125 to 0.3125
- gain: bfloat16 [4096], replicated, may hold values from 0.099609375 to 1.8984375
- expert_ids: int32 [2304, 2], P('branch'), may hold values from 0 to 11, all different within a row; in each aligned block of 192 rows (0 to 191, 192 to 383, ...) at most 40 rows name the same one
- combine_codes: int32 [2304, 2], P('branch'), may hold values from 1 to 63
- gate_weight: bfloat16 [12, 4096, 8192], P('branch', None, 'shard'), may hold values from -0.09375 to 0.09375
- up_weight: bfloat16 [12, 4096, 8192], P('branch', None, 'shard'), may hold values from -0.09375 to 0.09375
- down_weight: bfloat16 [12, 8192, 4096], P('branch', 'shard'), may hold values from -0.1875 to 0.1875
Outputs:
- mixed: bfloat16 [2304, 4096], P('branch', 'shard')
- merged_weight: bfloat16 [4096, 4096], P(None, 'shard')
The draws below stay inside these ranges and needn't reach their ends.
Inputs may be any that keep to these rules, and one draw needn't show every extreme that they name: `expert_ids`: each token names two different experts. Among the 192 tokens of one branch no expert is named more than 40 times, a bound that some block reaches.
All inputs are finite; a program needn't handle non-finite values.
Results may differ from the reference program's by a relative error of at most 0.022.
Values may be sent and summed in bfloat16 or wider, within the bound.
No kernel may reach another device: no remote copies, remote signals or barrier semaphores. Data moves between devices by JAX's collectives and lax.ppermute only.
A program may use at most 64 MiB of HBM per device.

```python
import math
import jax
import jax.numpy as jnp
import numpy as np
from jax import lax

D = 4096
FF = 8192
TOK_BR = 192
EXPERTS = 12
CAP = 40
TOKENS = 2304


def place_ends(array, own_key, least, top_value):
    spot = [jax.random.randint(jax.random.fold_in(own_key, axis), (), 0, length) for axis, length in enumerate(array.shape)]
    main_axis = array.shape.index(max(array.shape))
    neighbour = spot[:main_axis] + [(spot[main_axis] + 1) % array.shape[main_axis]] + spot[main_axis + 1:]
    return array.at[tuple(spot)].set(least).at[tuple(neighbour)].set(top_value)


def spiked(entries, key, source, target, parts, factor):
    def block_of(axis_at):
        return (jnp.arange(entries.shape[axis_at]) // (entries.shape[axis_at] // parts)).reshape((-1,) + (1,) * (entries.ndim - 1 - axis_at))

    first = jax.random.permutation(key, parts)[block_of(target)]
    other_side = (block_of(target) + parts // 2) % parts
    return jnp.where((block_of(source) == first) | (block_of(source) == other_side), factor * entries, entries)


def block_scale(rng, extent, shards, low, top_value):
    def one(axis_at, shards_of):
        heights = jax.random.uniform(jax.random.fold_in(jax.random.fold_in(rng, 6), axis_at), (shards_of,), jnp.float32, low / len(shards), top_value / len(shards))
        return jnp.repeat(jnp.exp(heights), extent[axis_at] // shards_of).reshape((-1,) + (1,) * (len(extent) - axis_at - 1))

    loudness = one(*shards[0])
    for cut in shards[1:]:
        loudness = loudness * one(*cut)
    return loudness


def shared_out(key, own, number, rows, count, top, bound, skew):
    ranking = jax.random.permutation(key, count)
    packed, usual = shares(count, rows * top, bound, skew, True), shares(count, rows * top, bound, skew, False)
    places = jnp.arange(count)

    def named(lengths, offset_by):
        used = int((lengths > 0).sum())
        fixed = max(1, used // 4)
        passed = fixed + (places - fixed + offset_by * (used - fixed)) % max(1, count - fixed)
        return jnp.zeros((count,), jnp.int32).at[ranking[jnp.where(places < fixed, places, passed)]].set(jnp.asarray(lengths, jnp.int32))

    lengths = jnp.where(number % 4 == 0, named(packed, number // 4), named(usual, number - number // 4 - 1))
    mixed = jax.random.permutation(jax.random.fold_in(own, 3), count)
    donor, taker = mixed[0:count // 2 * 2:2], mixed[1:count // 2 * 2:2]
    room = jnp.minimum(lengths[donor] - 1, bound - lengths[taker]) // 2
    room = jnp.where((donor == ranking[0]) | (taker == ranking[0]) | (lengths[taker] == 0), 0, jnp.maximum(room, 0))
    passed = jax.random.randint(jax.random.fold_in(own, 4), (count // 2,), 0, 1 << 20) % (room + 1)
    lengths = lengths.at[donor].add(-passed).at[taker].add(passed)
    labels = jnp.searchsorted(jnp.cumsum(lengths), jnp.arange(rows * top), side="right").astype(jnp.int32)
    table = labels.reshape(top, rows).T
    table = table[jax.random.permutation(jax.random.fold_in(own, 1), rows)]
    offset_by = jax.random.randint(jax.random.fold_in(own, 2), (rows, 1), 0, top)
    return jnp.take_along_axis(table, (jnp.arange(top)[None, :] + offset_by) % top, axis=1)


def shares(amount, total, limit, skew, full):
    weights = [(1 << 20) // math.isqrt(standing ** skew) + 1 for standing in range(1, amount + 1)]
    largest = limit if full else min(limit, max(-(-total // amount), total * weights[0] // sum(weights)))
    least = 1 if total - largest >= amount - 1 else 0
    holding, surplus = [largest] + [least] * (amount - 1), total - largest - least * (amount - 1)
    while surplus > 0:
        movable = [i for i in range(1, amount) if holding[i] < largest] or [i for i in range(1, amount) if holding[i] < limit]
        pool, budget = sum([weights[i] for i in movable]), surplus
        for i in movable:
            extra = min(limit - holding[i], max(1, budget * weights[i] // pool), surplus)
            holding[i] = holding[i] + extra
            surplus = surplus - extra
    return np.array(holding)


def normal_values(key, shape, width, limit, split=(), kind=jnp.bfloat16):
    level = block_scale(key, shape, split, -0.22, 0.18) if split else 1.0
    result = jax.random.normal(key, shape, jnp.float32) * width * level
    return jnp.minimum(jnp.maximum(result, -limit), limit).astype(kind)


def bell_draw_with(key, shape, spread, bound, cuts, heavy, held_as=jnp.bfloat16):
    values = spread * jax.random.normal(key, shape, jnp.float32)
    if cuts:
        values = values * block_scale(key, shape, cuts, -0.22, 0.18)
    return jnp.clip(spiked(values, jax.random.fold_in(key, 3), *heavy), -bound, bound).astype(held_as)


def setup_inputs(seed: int = 0) -> dict:
    key_of = jax.random.split(jax.random.key(seed), 10)
    resid = normal_values(key_of[0], (TOKENS, D), 1.0, 6.0, ((0, 12), (1, 64)))
    context = normal_values(key_of[1], (TOKENS, D), 1.0, 6.0, ((0, 12),))
    o_weight = normal_values(key_of[2], (EXPERTS, D, D), (D // EXPERTS) ** -0.5, 0.3125, ((0, 12), (2, 64)))
    gain = jnp.clip(1.0 + 0.18 * jax.random.normal(key_of[3], (D,), jnp.float32), 0.099609375, 1.8984375).astype(jnp.bfloat16)
    expert_ids_keys = jax.random.split(jax.random.fold_in(key_of[4], 1), TOKENS // TOK_BR)
    expert_ids_turns = jax.random.permutation(jax.random.fold_in(key_of[4], 3), TOKENS // TOK_BR)
    expert_ids = jax.vmap(lambda own, number: shared_out(jax.random.fold_in(key_of[4], 2), own, number, TOK_BR, EXPERTS, 2, CAP, 2))(expert_ids_keys, expert_ids_turns).reshape((TOKENS, 2))
    combine_codes = place_ends(jax.random.randint(key_of[5], (TOKENS, 2), 1, 64), jax.random.fold_in(key_of[5], 1), 1, 63).astype(jnp.int32)
    gate_weight = normal_values(key_of[6], (EXPERTS, D, FF), D ** -0.5, 0.09375, ((0, 12), (2, 64)))
    up_weight = normal_values(key_of[7], (EXPERTS, D, FF), D ** -0.5, 0.09375, ((0, 12), (2, 64)))
    down_weight = bell_draw_with(key_of[8], (EXPERTS, FF, D), FF ** -0.5, 0.1875, ((0, 12), (1, 64)), (1, 2, 64, 4.0))
    return dict(resid=resid, context=context, o_weight=o_weight, gain=gain, expert_ids=expert_ids, combine_codes=combine_codes, gate_weight=gate_weight, up_weight=up_weight, down_weight=down_weight)


epsilon = 1e-05

def slot_index(route_rows):
    flat_ids = route_rows.reshape(-1)
    onehot = (flat_ids[:, None] == jnp.arange(EXPERTS, dtype=jnp.int32)[None, :]).astype(jnp.int32)
    before = jnp.cumsum(onehot, axis=0) - onehot
    position = lax.optimization_barrier(jnp.sum(before * onehot, axis=1))
    return (flat_ids * CAP + position).astype(jnp.int32)

def fill_slots(branch_rows, slots):
    repeated = jnp.repeat(branch_rows, 2, axis=0)
    return jnp.zeros((EXPERTS * CAP, D), jnp.bfloat16).at[slots].set(repeated)

def run_expert(operands):
    inputs, w_gate, w_up, w_down = operands
    gate_acts = jnp.dot(inputs, w_gate, preferred_element_type=jnp.float32)
    up_acts = jnp.dot(inputs, w_up, preferred_element_type=jnp.float32)
    inner = (jax.nn.silu(gate_acts) * up_acts).astype(jnp.bfloat16)
    return jnp.dot(inner, w_down, preferred_element_type=jnp.float32).astype(jnp.bfloat16)

def reference(resid, context, o_weight, gain, expert_ids, combine_codes, gate_weight, up_weight, down_weight):
    merged = (lax.optimization_barrier(jnp.sum(o_weight.astype(jnp.float32), axis=0)) / EXPERTS).astype(jnp.bfloat16)
    hidden_state = (resid.astype(jnp.float32) + jnp.dot(context, merged, preferred_element_type=jnp.float32)).astype(jnp.bfloat16)
    state_f = hidden_state.astype(jnp.float32)
    mean_sq = lax.optimization_barrier(jnp.mean(state_f * state_f, axis=1, keepdims=True))
    normed = (state_f * lax.rsqrt(mean_sq + epsilon) * gain.astype(jnp.float32)[None, :]).astype(jnp.bfloat16)
    slots = jax.vmap(slot_index)(expert_ids.reshape(EXPERTS, TOK_BR, 2))
    sent_rows = jax.vmap(fill_slots)(normed.reshape(EXPERTS, TOK_BR, D), slots)
    arrived = sent_rows.reshape(EXPERTS, EXPERTS, CAP, D).transpose(1, 0, 2, 3).reshape(EXPERTS, EXPERTS * CAP, D)
    expert_out = lax.map(run_expert, (arrived, gate_weight, up_weight, down_weight))
    returned = expert_out.reshape(EXPERTS, EXPERTS, CAP, D).transpose(1, 0, 2, 3).reshape(EXPERTS, EXPERTS * CAP, D)
    picked = jax.vmap(lambda source, where: source[where])(returned, slots)
    picked = picked.reshape(EXPERTS, TOK_BR, 2, D).astype(jnp.float32)
    code_vals = combine_codes.astype(jnp.float32).reshape(EXPERTS, TOK_BR, 2)
    mix_weights = code_vals / lax.optimization_barrier(jnp.sum(code_vals, axis=2, keepdims=True))
    mixture = lax.optimization_barrier(jnp.sum(picked * mix_weights[:, :, :, None], axis=2))
    mixed = (state_f.reshape(EXPERTS, TOK_BR, D) + mixture).reshape(TOKENS, D).astype(jnp.bfloat16)
    return (mixed, merged)
```

```python
import jax
import jax.numpy as jnp
from jax import lax
from jax.experimental import pallas as pl
from jax.experimental.pallas import tpu as pltpu
from jax.sharding import Mesh, PartitionSpec as P

epsilon = 1e-05
MEMBERS = 4
RING = 8
SHARD = ("group", "chip", "core")
LANES = 128
BF16 = jnp.bfloat16
F32 = jnp.float32


def expert_kernel(x_ref, gain_ref, *refs):
    given, out_ref, rows_ref, weights, sems = refs[:MEMBERS], *refs[MEMBERS:]

    def fetch(m, kind):
        return pltpu.make_async_copy(given[m].at[kind], weights.at[m, kind], sems.at[m, kind])

    for m in range(MEMBERS):
        fetch(m, 0).start()
        fetch(m, 1).start()
    for m in range(MEMBERS):
        fetch(m, 2).start()
    sources, half, _ = x_ref.shape
    width = rows_ref.shape[1]
    low = lax.broadcasted_iota(jnp.int32, (half, LANES), 1) < LANES // 2
    squares = [jnp.zeros((half, LANES), F32), jnp.zeros((half, LANES), F32)]
    for q in range(sources // 2):
        even, odd = x_ref[2 * q].astype(F32), x_ref[2 * q + 1].astype(F32)
        top = jnp.where(low, even, pltpu.roll(odd, LANES // 2, 1))
        bottom = jnp.where(low, pltpu.roll(even, LANES // 2, 1), odd)
        squares[0] += top * top
        squares[1] += bottom * bottom
        rows_ref[:half, q * LANES : (q + 1) * LANES] = top.astype(BF16)
        rows_ref[half:, q * LANES : (q + 1) * LANES] = bottom.astype(BF16)
    total = jnp.sum(jnp.concatenate(squares, axis=0), axis=1, keepdims=True)
    inverse = lax.rsqrt(total / width + epsilon)
    chunk = 2 * LANES
    for k in range(0, width, chunk):
        gain = gain_ref[:, k : k + chunk]
        rows_ref[:, k : k + chunk] = (rows_ref[:, k : k + chunk].astype(F32) * inverse * gain).astype(BF16)
    inner = []
    for m in range(MEMBERS):
        fetch(m, 0).wait()
        fetch(m, 1).wait()
        acts = jnp.zeros((2 * half, 2 * LANES), F32)
        for k in range(0, width, chunk):
            both = jnp.concatenate([weights[m, 0, k : k + chunk, :], weights[m, 1, k : k + chunk, :]], axis=1)
            acts += jnp.dot(rows_ref[:, k : k + chunk], both, preferred_element_type=F32)
        gate_acts, up_acts = acts[:, :LANES], acts[:, LANES:]
        inner.append((gate_acts / (1.0 + jnp.exp(-gate_acts)) * up_acts).astype(BF16))
    inner = jnp.concatenate(inner, axis=1)
    for m in range(MEMBERS):
        fetch(m, 2).wait()
    for q in range(0, width // LANES, 2):
        columns = [
            jnp.concatenate([weights[m, 2, (q + j) * LANES : (q + j + 1) * LANES, :] for m in range(MEMBERS)], axis=0)
            for j in range(2)
        ]
        part = jnp.dot(inner, jnp.concatenate(columns, axis=1), preferred_element_type=F32)
        for j in range(2):
            s = 2 * (q + j)
            top = part[:half, j * LANES : (j + 1) * LANES]
            bottom = part[half:, j * LANES : (j + 1) * LANES]
            out_ref[s] = jnp.where(low, top, pltpu.roll(bottom, LANES // 2, 1)).astype(BF16)
            out_ref[s + 1] = jnp.where(low, pltpu.roll(top, LANES // 2, 1), bottom).astype(BF16)


def run_expert(x, gain, weights):
    sources, half, _ = x.shape
    width = gain.shape[1]
    size = sum(w.size for w in weights)
    return pl.pallas_call(
        expert_kernel,
        out_shape=jax.ShapeDtypeStruct(x.shape, BF16),
        in_specs=[pl.BlockSpec(memory_space=pltpu.VMEM)] * 2 + [pl.BlockSpec(memory_space=pl.ANY)] * MEMBERS,
        out_specs=pl.BlockSpec(memory_space=pltpu.VMEM),
        scratch_shapes=[
            pltpu.VMEM((2 * half, width), BF16),
            pltpu.VMEM((MEMBERS,) + weights[0].shape, BF16),
            pltpu.SemaphoreType.DMA((MEMBERS, 3)),
        ],
        compiler_params=pltpu.CompilerParams(vmem_limit_bytes=56 * 1024 * 1024),
        cost_estimate=pl.CostEstimate(
            flops=2 * 2 * half * size, bytes_accessed=2 * (2 * x.size + size), transcendentals=0
        ),
    )(x, gain, *weights)


def ring_pairs(shards):
    pairs = []
    for source in range(shards):
        line, place, core = source // (2 * RING), source // 2 % RING, source % 2
        step = 1 if place % 2 == core else RING - 1
        pairs.append((source, (line * RING + (place + step) % RING) * 2 + core))
    return pairs


def slot_index(route_rows, n_experts, capacity):
    flat_ids = route_rows.reshape(-1)
    count = flat_ids.shape[0]
    onehot = flat_ids[:, None] == jnp.arange(n_experts, dtype=jnp.int32)[None, :]
    order = jnp.arange(count, dtype=jnp.int32)
    earlier = (order[:, None] > order[None, :]).astype(BF16)
    before = jnp.dot(earlier, onehot.astype(BF16), preferred_element_type=F32)
    position = jnp.sum(jnp.where(onehot, before, 0.0), axis=1).astype(jnp.int32)
    return (flat_ids * capacity + position).reshape(route_rows.shape)


def local(
    resid, context, o_weight, gain, expert_ids, combine_codes, gate_weight, up_weight, down_weight
):
    n_experts = lax.axis_size("branch")
    n_groups = lax.axis_size("group")
    shards = n_groups * MEMBERS
    tok_rows, feat_width = resid.shape
    full_width = context.shape[1]
    capacity = 5 * tok_rows // (2 * n_experts)
    half_cap = capacity // 2
    quarter = n_experts // MEMBERS * half_cap
    half = -(-quarter // 16) * 16

    blocks = down_weight[0].reshape(-1, full_width // LANES, LANES).transpose(1, 0, 2).reshape(full_width, LANES)
    own = jnp.stack([gate_weight[0], up_weight[0], blocks])
    beside = lax.ppermute(own, SHARD, ring_pairs(shards))
    own_core = lax.ppermute(own, "core", [(0, 1), (1, 0)])

    piece = -(-full_width // (LANES * n_experts)) * LANES
    missing = n_experts * piece - full_width
    columns = jnp.pad(o_weight[0].T, ((0, 0), (0, missing))).reshape(feat_width, n_experts, piece)
    parts = lax.all_to_all(columns.transpose(1, 0, 2), "branch", 0, 0, tiled=True)
    mean_part = (jnp.sum(parts.astype(F32), axis=0) / n_experts).astype(BF16)
    spread = jnp.broadcast_to(mean_part[None], (n_experts, feat_width, piece))
    merged = lax.all_to_all(spread, "branch", 0, 0, tiled=True)
    merged = merged.transpose(1, 0, 2).reshape(feat_width, n_experts * piece)[:, :full_width].T

    hidden_state = (
        resid.astype(F32) + jnp.dot(context, merged, preferred_element_type=F32)
    ).astype(BF16)

    hidden_state, beside = lax.optimization_barrier((hidden_state, beside))
    beside_core = lax.ppermute(beside, "core", [(0, 1), (1, 0)])

    slots = slot_index(expert_ids, n_experts, capacity)
    all_slots = jnp.arange(n_experts * capacity, dtype=jnp.int32)
    pick_table = ((slots[None, :, 0] == all_slots[:, None]) | (slots[None, :, 1] == all_slots[:, None])).astype(BF16)
    sent = jnp.dot(pick_table, hidden_state, preferred_element_type=F32).astype(BF16)
    sent = sent.reshape(n_experts, 2, half_cap, feat_width)
    sent = jnp.concatenate([sent[:, 0], sent[:, 1]], axis=2)
    arrived = lax.all_to_all(sent, "branch", 0, 0, tiled=True)

    quarters = jnp.pad(arrived.reshape(MEMBERS, quarter, LANES), ((0, 0), (0, half - quarter), (0, 0)))
    copies = jnp.broadcast_to(quarters[None], (n_groups, MEMBERS, half, LANES)).reshape(shards, half, LANES)
    gathered = lax.all_to_all(copies, SHARD, 0, 0, tiled=True)
    partial_out = run_expert(gathered, gain.astype(F32).reshape(1, -1), (own, own_core, beside, beside_core))
    exchanged = lax.all_to_all(partial_out, SHARD, 0, 0, tiled=True)
    expert_out = jnp.sum(exchanged.reshape(n_groups, MEMBERS, half, LANES).astype(F32), axis=0).astype(BF16)

    expert_out = expert_out[:, :quarter].reshape(n_experts, half_cap, LANES)
    returned = lax.all_to_all(expert_out, "branch", 0, 0, tiled=True)
    returned = jnp.stack([returned[:, :, :feat_width], returned[:, :, feat_width:]], axis=1)
    returned = returned.reshape(n_experts * capacity, feat_width)
    code_vals = combine_codes.astype(F32)
    mix_weights = code_vals / jnp.sum(code_vals, axis=1, keepdims=True)
    mixture = jnp.zeros((tok_rows, feat_width), F32)
    for k in range(2):
        table = (slots[:, k, None] == all_slots[None, :]).astype(BF16)
        picked = jnp.dot(table, returned, preferred_element_type=F32)
        mixture += picked * mix_weights[:, k, None]
    mixed = (hidden_state.astype(F32) + mixture).astype(BF16)
    return (mixed, merged)


def solution(mesh):
    n_branches, n_shards = mesh.devices.shape
    fine = Mesh(mesh.devices.reshape(n_branches, n_shards // MEMBERS, 2, 2), ("branch",) + SHARD)
    in_specs = (
        P("branch", SHARD),
        P("branch", None),
        P("branch", None, SHARD),
        P(),
        P("branch", None),
        P("branch", None),
        P("branch", None, SHARD),
        P("branch", None, SHARD),
        P("branch", SHARD, None),
    )
    out_specs = (P("branch", SHARD), P(None, SHARD))
    return jax.shard_map(local, mesh=fine, in_specs=in_specs, out_specs=out_specs, check_vma=False)
```

```python
import functools

import jax
import jax.numpy as jnp
from jax import lax
from jax.experimental import pallas as pl
from jax.experimental.pallas import tpu as pltpu
from jax.sharding import Mesh, PartitionSpec as P

epsilon = 1e-05
MEMBERS = 4
ROWS = 16
SLOT_ROWS = 32
RING = 8
SHARD = ("group", "chip", "core")
LANES = 128
BF16 = jnp.bfloat16
F32 = jnp.float32


def expert_kernel(x_ref, gain_ref, *refs):
    given, out_ref, rows_ref, weights, sems = refs[:MEMBERS], *refs[MEMBERS:]

    def fetch(m, kind):
        return pltpu.make_async_copy(given[m].at[kind], weights.at[m, kind], sems.at[m, kind])

    for m in range(MEMBERS):
        fetch(m, 0).start()
        fetch(m, 1).start()
    for m in range(MEMBERS):
        fetch(m, 2).start()
    sources, half, _ = x_ref.shape
    width = rows_ref.shape[1]
    low = lax.broadcasted_iota(jnp.int32, (half, LANES), 1) < LANES // 2
    squares = [jnp.zeros((half, LANES), F32), jnp.zeros((half, LANES), F32)]
    for q in range(sources // 2):
        even, odd = x_ref[2 * q].astype(F32), x_ref[2 * q + 1].astype(F32)
        top = jnp.where(low, even, pltpu.roll(odd, LANES // 2, 1))
        bottom = jnp.where(low, pltpu.roll(even, LANES // 2, 1), odd)
        squares[0] += top * top
        squares[1] += bottom * bottom
        rows_ref[:half, q * LANES : (q + 1) * LANES] = top.astype(BF16)
        rows_ref[half:, q * LANES : (q + 1) * LANES] = bottom.astype(BF16)
    total = jnp.sum(jnp.concatenate(squares, axis=0), axis=1, keepdims=True)
    inverse = lax.rsqrt(total / width + epsilon)
    chunk = 2 * LANES
    for k in range(0, width, chunk):
        gain = gain_ref[:, k : k + chunk]
        rows_ref[:, k : k + chunk] = (rows_ref[:, k : k + chunk].astype(F32) * inverse * gain).astype(BF16)
    inner = []
    for m in range(MEMBERS):
        fetch(m, 0).wait()
        fetch(m, 1).wait()
        acts = jnp.zeros((2 * half, 2 * LANES), F32)
        for k in range(0, width, chunk):
            both = jnp.concatenate([weights[m, 0, k : k + chunk, :], weights[m, 1, k : k + chunk, :]], axis=1)
            acts += jnp.dot(rows_ref[:, k : k + chunk], both, preferred_element_type=F32)
        gate_acts, up_acts = acts[:, :LANES], acts[:, LANES:]
        inner.append((gate_acts / (1.0 + jnp.exp(-gate_acts)) * up_acts).astype(BF16))
    inner = jnp.concatenate(inner, axis=1)
    for m in range(MEMBERS):
        fetch(m, 2).wait()
    for q in range(0, width // LANES, 2):
        columns = [
            jnp.concatenate([weights[m, 2, (q + j) * LANES : (q + j + 1) * LANES, :] for m in range(MEMBERS)], axis=0)
            for j in range(2)
        ]
        part = jnp.dot(inner, jnp.concatenate(columns, axis=1), preferred_element_type=F32)
        for j in range(2):
            s = 2 * (q + j)
            top = part[:half, j * LANES : (j + 1) * LANES]
            bottom = part[half:, j * LANES : (j + 1) * LANES]
            out_ref[s] = jnp.where(low, top, pltpu.roll(bottom, LANES // 2, 1)).astype(BF16)
            out_ref[s + 1] = jnp.where(low, pltpu.roll(top, LANES // 2, 1), bottom).astype(BF16)


def run_expert(x, gain, weights):
    sources, half, _ = x.shape
    width = gain.shape[1]
    size = sum(w.size for w in weights)
    return pl.pallas_call(
        expert_kernel,
        out_shape=jax.ShapeDtypeStruct(x.shape, BF16),
        in_specs=[pl.BlockSpec(memory_space=pltpu.VMEM)] * 2 + [pl.BlockSpec(memory_space=pl.ANY)] * MEMBERS,
        out_specs=pl.BlockSpec(memory_space=pltpu.VMEM),
        scratch_shapes=[
            pltpu.VMEM((2 * half, width), BF16),
            pltpu.VMEM((MEMBERS,) + weights[0].shape, BF16),
            pltpu.SemaphoreType.DMA((MEMBERS, 3)),
        ],
        compiler_params=pltpu.CompilerParams(vmem_limit_bytes=56 * 1024 * 1024),
        cost_estimate=pl.CostEstimate(
            flops=2 * 2 * half * size, bytes_accessed=2 * (2 * x.size + size), transcendentals=0
        ),
    )(x, gain, *weights)


def tile_of(number, width):
    across = width // LANES
    row, column = number // across * ROWS, number % across * LANES
    return slice(row, row + ROWS), slice(column, column + LANES)


def cut_kernel(columns_ref, out_ref):
    feats, width = columns_ref.shape
    tiles = feats // ROWS * (width // LANES)
    for t in range(tiles):
        rows, lanes = tile_of(t, width)
        out_ref[t * ROWS : (t + 1) * ROWS, :] = columns_ref[rows, lanes]
    if tiles * ROWS < out_ref.shape[0]:
        out_ref[tiles * ROWS :, :] = jnp.zeros((out_ref.shape[0] - tiles * ROWS, LANES), BF16)


def cut(columns, out_rows):
    return pl.pallas_call(
        cut_kernel,
        out_shape=jax.ShapeDtypeStruct((out_rows, LANES), BF16),
        in_specs=[pl.BlockSpec(memory_space=pltpu.VMEM)],
        out_specs=pl.BlockSpec(memory_space=pltpu.VMEM),
        cost_estimate=pl.CostEstimate(flops=0, bytes_accessed=4 * columns.size, transcendentals=0),
    )(columns)


def hidden_kernel(half_cap, parts_ref, context_ref, resid_ref, slots_ref, merged_ref, hidden_ref, sent_ref):
    feats, width = merged_ref.shape
    tokens = context_ref.shape[0]
    for t in range(feats // ROWS * (width // LANES)):
        rows, lanes = tile_of(t, width)
        merged_ref[rows, lanes] = parts_ref[t * ROWS : (t + 1) * ROWS, :]
    across = (((1,), (1,)), ((), ()))
    product = lax.dot_general(merged_ref[...], context_ref[...], across, preferred_element_type=F32)
    hidden = (resid_ref[...].astype(F32) + product).astype(BF16)
    hidden_ref[...] = hidden
    count = sent_ref.shape[0]
    row = lax.broadcasted_iota(jnp.int32, (count, tokens), 0)
    place, expert = row % SLOT_ROWS, row // SLOT_ROWS
    empty = jnp.zeros((LANES - feats, tokens), BF16)
    sent = jnp.zeros((count, LANES), F32)
    for side in range(2):
        slot = jnp.where(place < half_cap, (2 * expert + side) * half_cap + place, -1)
        table = ((slots_ref[0:1, :] == slot) | (slots_ref[1:2, :] == slot)).astype(F32).astype(BF16)
        lanes = jnp.concatenate([hidden, empty] if side == 0 else [empty, hidden], axis=0)
        sent += lax.dot_general(table, lanes, across, preferred_element_type=F32)
    sent_ref[...] = sent.astype(BF16)


def hidden_rows(parts, context, resid, slots, n_experts, half_cap):
    feats, tokens = resid.shape
    width = context.shape[1]
    return pl.pallas_call(
        functools.partial(hidden_kernel, half_cap),
        out_shape=(
            jax.ShapeDtypeStruct((feats, width), BF16),
            jax.ShapeDtypeStruct((feats, tokens), BF16),
            jax.ShapeDtypeStruct((n_experts * SLOT_ROWS, LANES), BF16),
        ),
        in_specs=[pl.BlockSpec(memory_space=pltpu.VMEM)] * 4,
        out_specs=[pl.BlockSpec(memory_space=pltpu.VMEM)] * 3,
        cost_estimate=pl.CostEstimate(
            flops=2 * feats * tokens * width, bytes_accessed=2 * (2 * feats + tokens) * width, transcendentals=0
        ),
    )(parts, context, resid, slots)


def ring_pairs(shards):
    pairs = []
    for source in range(shards):
        line, place, core = source // (2 * RING), source // 2 % RING, source % 2
        step = 1 if place % 2 == core else RING - 1
        pairs.append((source, (line * RING + (place + step) % RING) * 2 + core))
    return pairs


def slot_index(route_rows, n_experts, capacity):
    flat_ids = route_rows.reshape(-1)
    count = flat_ids.shape[0]
    onehot = flat_ids[:, None] == jnp.arange(n_experts, dtype=jnp.int32)[None, :]
    order = jnp.arange(count, dtype=jnp.int32)
    earlier = (order[:, None] > order[None, :]).astype(BF16)
    before = jnp.dot(earlier, onehot.astype(BF16), preferred_element_type=F32)
    position = jnp.sum(jnp.where(onehot, before, 0.0), axis=1).astype(jnp.int32)
    return (flat_ids * capacity + position).reshape(route_rows.shape)


def local(
    resid, context, o_weight, gain, expert_ids, combine_codes, gate_weight, up_weight, down_weight
):
    n_experts = lax.axis_size("branch")
    n_groups = lax.axis_size("group")
    shards = n_groups * MEMBERS
    tok_rows, feat_width = resid.shape
    full_width = context.shape[1]
    capacity = 5 * tok_rows // (2 * n_experts)
    half_cap = capacity // 2
    quarter = n_experts // MEMBERS * half_cap
    half = -(-quarter // 16) * 16

    blocks = down_weight[0].reshape(-1, full_width // LANES, LANES).transpose(1, 0, 2).reshape(full_width, LANES)
    own = jnp.stack([gate_weight[0], up_weight[0], blocks])
    beside = lax.ppermute(own, SHARD, ring_pairs(shards))
    own_core = lax.ppermute(own, "core", [(0, 1), (1, 0)])

    piece = -(-(full_width * feat_width) // (LANES * ROWS * n_experts)) * ROWS
    tiles = cut(o_weight[0].T, n_experts * piece).reshape(n_experts, piece, LANES)
    parts = lax.all_to_all(tiles, "branch", 0, 0, tiled=True)
    mean_part = (jnp.sum(parts.astype(F32), axis=0) / n_experts).astype(BF16)
    spread = jnp.broadcast_to(mean_part[None], (n_experts, piece, LANES))
    all_parts = lax.all_to_all(spread, "branch", 0, 0, tiled=True).reshape(n_experts * piece, LANES)

    slots = slot_index(expert_ids, n_experts, capacity)
    merged, hidden, sent = hidden_rows(all_parts, context, resid.T, slots.T, n_experts, half_cap)
    merged, hidden_state = merged.T, hidden.T
    hidden_state, beside = lax.optimization_barrier((hidden_state, beside))
    beside_core = lax.ppermute(beside, "core", [(0, 1), (1, 0)])
    arrived = lax.all_to_all(sent.reshape(n_experts, SLOT_ROWS, LANES), "branch", 0, 0, tiled=True)
    arrived = arrived[:, :half_cap]

    quarters = jnp.pad(arrived.reshape(MEMBERS, quarter, LANES), ((0, 0), (0, half - quarter), (0, 0)))
    copies = jnp.broadcast_to(quarters[None], (n_groups, MEMBERS, half, LANES)).reshape(shards, half, LANES)
    gathered = lax.all_to_all(copies, SHARD, 0, 0, tiled=True)
    partial_out = run_expert(gathered, gain.astype(F32).reshape(1, -1), (own, own_core, beside, beside_core))
    exchanged = lax.all_to_all(partial_out, SHARD, 0, 0, tiled=True)
    expert_out = jnp.sum(exchanged.reshape(n_groups, MEMBERS, half, LANES).astype(F32), axis=0).astype(BF16)

    expert_out = expert_out[:, :quarter].reshape(n_experts, half_cap, LANES)
    returned = lax.all_to_all(expert_out, "branch", 0, 0, tiled=True)
    returned = jnp.stack([returned[:, :, :feat_width], returned[:, :, feat_width:]], axis=1)
    returned = returned.reshape(n_experts * capacity, feat_width)
    all_slots = jnp.arange(n_experts * capacity, dtype=jnp.int32)
    code_vals = combine_codes.astype(F32)
    mix_weights = code_vals / jnp.sum(code_vals, axis=1, keepdims=True)
    mixture = jnp.zeros((tok_rows, feat_width), F32)
    for k in range(2):
        table = (slots[:, k, None] == all_slots[None, :]).astype(BF16)
        picked = jnp.dot(table, returned, preferred_element_type=F32)
        mixture += picked * mix_weights[:, k, None]
    mixed = (hidden_state.astype(F32) + mixture).astype(BF16)
    return (mixed, merged)


def solution(mesh):
    n_branches, n_shards = mesh.devices.shape
    fine = Mesh(mesh.devices.reshape(n_branches, n_shards // MEMBERS, 2, 2), ("branch",) + SHARD)
    in_specs = (
        P("branch", SHARD),
        P("branch", None),
        P("branch", None, SHARD),
        P(),
        P("branch", None),
        P("branch", None),
        P("branch", None, SHARD),
        P("branch", None, SHARD),
        P("branch", SHARD, None),
    )
    out_specs = (P("branch", SHARD), P(None, SHARD))
    return jax.shard_map(local, mesh=fine, in_specs=in_specs, out_specs=out_specs, check_vma=False)
```

```python
import functools

import jax
import jax.numpy as jnp
from jax import lax
from jax.experimental import pallas as pl
from jax.experimental.pallas import tpu as pltpu
from jax.sharding import Mesh, PartitionSpec as P

epsilon = 1e-05
MEMBERS = 4
ROWS = 16
SLOT_ROWS = 32
RING = 8
SHARD = ("group", "chip", "core")
LANES = 128
BF16 = jnp.bfloat16
F32 = jnp.float32


def expert_kernel(x_ref, gain_ref, *refs):
    given, out_ref, rows_ref, weights, sems = refs[:MEMBERS], *refs[MEMBERS:]

    def fetch(m, kind):
        return pltpu.make_async_copy(given[m].at[kind], weights.at[m, kind], sems.at[m, kind])

    for m in range(MEMBERS):
        fetch(m, 0).start()
        fetch(m, 1).start()
    for m in range(MEMBERS):
        fetch(m, 2).start()
    sources, half, _ = x_ref.shape
    width = rows_ref.shape[1]
    low = lax.broadcasted_iota(jnp.int32, (half, LANES), 1) < LANES // 2
    squares = [jnp.zeros((half, LANES), F32), jnp.zeros((half, LANES), F32)]
    for q in range(sources // 2):
        even, odd = x_ref[2 * q].astype(F32), x_ref[2 * q + 1].astype(F32)
        top = jnp.where(low, even, pltpu.roll(odd, LANES // 2, 1))
        bottom = jnp.where(low, pltpu.roll(even, LANES // 2, 1), odd)
        squares[0] += top * top
        squares[1] += bottom * bottom
        rows_ref[:half, q * LANES : (q + 1) * LANES] = top.astype(BF16)
        rows_ref[half:, q * LANES : (q + 1) * LANES] = bottom.astype(BF16)
    total = jnp.sum(jnp.concatenate(squares, axis=0), axis=1, keepdims=True)
    inverse = lax.rsqrt(total / width + epsilon)
    chunk = 2 * LANES
    for k in range(0, width, chunk):
        gain = gain_ref[:, k : k + chunk]
        rows_ref[:, k : k + chunk] = (rows_ref[:, k : k + chunk].astype(F32) * inverse * gain).astype(BF16)
    inner = []
    for m in range(MEMBERS):
        fetch(m, 0).wait()
        fetch(m, 1).wait()
        acts = jnp.zeros((2 * half, 2 * LANES), F32)
        for k in range(0, width, chunk):
            both = jnp.concatenate([weights[m, 0, k : k + chunk, :], weights[m, 1, k : k + chunk, :]], axis=1)
            acts += jnp.dot(rows_ref[:, k : k + chunk], both, preferred_element_type=F32)
        gate_acts, up_acts = acts[:, :LANES], acts[:, LANES:]
        inner.append((gate_acts / (1.0 + jnp.exp(-gate_acts)) * up_acts).astype(BF16))
    inner = jnp.concatenate(inner, axis=1)
    for m in range(MEMBERS):
        fetch(m, 2).wait()
    for q in range(0, width // LANES, 2):
        columns = [
            jnp.concatenate([weights[m, 2, (q + j) * LANES : (q + j + 1) * LANES, :] for m in range(MEMBERS)], axis=0)
            for j in range(2)
        ]
        part = jnp.dot(inner, jnp.concatenate(columns, axis=1), preferred_element_type=F32)
        for j in range(2):
            s = 2 * (q + j)
            top = part[:half, j * LANES : (j + 1) * LANES]
            bottom = part[half:, j * LANES : (j + 1) * LANES]
            out_ref[s] = jnp.where(low, top, pltpu.roll(bottom, LANES // 2, 1)).astype(BF16)
            out_ref[s + 1] = jnp.where(low, pltpu.roll(top, LANES // 2, 1), bottom).astype(BF16)


def run_expert(x, gain, weights):
    sources, half, _ = x.shape
    width = gain.shape[1]
    size = sum(w.size for w in weights)
    return pl.pallas_call(
        expert_kernel,
        out_shape=jax.ShapeDtypeStruct(x.shape, BF16),
        in_specs=[pl.BlockSpec(memory_space=pltpu.VMEM)] * 2 + [pl.BlockSpec(memory_space=pl.ANY)] * MEMBERS,
        out_specs=pl.BlockSpec(memory_space=pltpu.VMEM),
        scratch_shapes=[
            pltpu.VMEM((2 * half, width), BF16),
            pltpu.VMEM((MEMBERS,) + weights[0].shape, BF16),
            pltpu.SemaphoreType.DMA((MEMBERS, 3)),
        ],
        compiler_params=pltpu.CompilerParams(vmem_limit_bytes=56 * 1024 * 1024),
        cost_estimate=pl.CostEstimate(
            flops=2 * 2 * half * size, bytes_accessed=2 * (2 * x.size + size), transcendentals=0
        ),
    )(x, gain, *weights)


def tile_of(number, width):
    across = width // LANES
    row, column = number // across * ROWS, number % across * LANES
    return slice(row, row + ROWS), slice(column, column + LANES)


def cut_kernel(columns_ref, out_ref):
    feats, width = columns_ref.shape
    tiles = feats // ROWS * (width // LANES)
    for t in range(tiles):
        rows, lanes = tile_of(t, width)
        out_ref[t * ROWS : (t + 1) * ROWS, :] = columns_ref[rows, lanes]
    if tiles * ROWS < out_ref.shape[0]:
        out_ref[tiles * ROWS :, :] = jnp.zeros((out_ref.shape[0] - tiles * ROWS, LANES), BF16)


def cut(columns, out_rows):
    return pl.pallas_call(
        cut_kernel,
        out_shape=jax.ShapeDtypeStruct((out_rows, LANES), BF16),
        in_specs=[pl.BlockSpec(memory_space=pltpu.VMEM)],
        out_specs=pl.BlockSpec(memory_space=pltpu.VMEM),
        cost_estimate=pl.CostEstimate(flops=0, bytes_accessed=4 * columns.size, transcendentals=0),
    )(columns)


def hidden_kernel(half_cap, parts_ref, context_ref, resid_ref, slots_ref, merged_ref, hidden_ref, sent_ref):
    feats, width = merged_ref.shape
    tokens = context_ref.shape[0]
    for t in range(feats // ROWS * (width // LANES)):
        rows, lanes = tile_of(t, width)
        merged_ref[rows, lanes] = parts_ref[t * ROWS : (t + 1) * ROWS, :]
    across = (((1,), (1,)), ((), ()))
    product = lax.dot_general(merged_ref[...], context_ref[...], across, preferred_element_type=F32)
    hidden = (resid_ref[...].astype(F32) + product).astype(BF16)
    hidden_ref[...] = hidden
    count = sent_ref.shape[0]
    row = lax.broadcasted_iota(jnp.int32, (count, tokens), 0)
    place, expert = row % SLOT_ROWS, row // SLOT_ROWS
    empty = jnp.zeros((LANES - feats, tokens), BF16)
    sent = jnp.zeros((count, LANES), F32)
    for side in range(2):
        slot = jnp.where(place < half_cap, (2 * expert + side) * half_cap + place, -1)
        table = ((slots_ref[0:1, :] == slot) | (slots_ref[1:2, :] == slot)).astype(F32).astype(BF16)
        lanes = jnp.concatenate([hidden, empty] if side == 0 else [empty, hidden], axis=0)
        sent += lax.dot_general(table, lanes, across, preferred_element_type=F32)
    sent_ref[...] = sent.astype(BF16)


def hidden_rows(parts, context, resid, slots, n_experts, half_cap):
    feats, tokens = resid.shape
    width = context.shape[1]
    return pl.pallas_call(
        functools.partial(hidden_kernel, half_cap),
        out_shape=(
            jax.ShapeDtypeStruct((feats, width), BF16),
            jax.ShapeDtypeStruct((feats, tokens), BF16),
            jax.ShapeDtypeStruct((n_experts * SLOT_ROWS, LANES), BF16),
        ),
        in_specs=[pl.BlockSpec(memory_space=pltpu.VMEM)] * 4,
        out_specs=[pl.BlockSpec(memory_space=pltpu.VMEM)] * 3,
        cost_estimate=pl.CostEstimate(
            flops=2 * feats * tokens * width, bytes_accessed=2 * (2 * feats + tokens) * width, transcendentals=0
        ),
    )(parts, context, resid, slots)


def combine_kernel(half_cap, returned_ref, hidden_ref, slots_ref, weights_ref, mixed_ref):
    feats, tokens = hidden_ref.shape
    count = returned_ref.shape[0]
    row = lax.broadcasted_iota(jnp.int32, (count, tokens), 0)
    place, expert = row % SLOT_ROWS, row // SLOT_ROWS
    down = (((0,), (0,)), ((), ()))
    mixed = hidden_ref[...].astype(F32)
    for k in range(2):
        picked = jnp.zeros((feats, tokens), F32)
        for side in range(2):
            slot = jnp.where(place < half_cap, (2 * expert + side) * half_cap + place, -1)
            table = (slots_ref[k : k + 1, :] == slot).astype(F32).astype(BF16)
            both = lax.dot_general(returned_ref[...], table, down, preferred_element_type=F32)
            picked += both[side * feats : (side + 1) * feats, :]
        mixed += picked * weights_ref[k : k + 1, :]
    mixed_ref[...] = mixed.astype(BF16)


def combine(returned, hidden, slots, weights, half_cap):
    return pl.pallas_call(
        functools.partial(combine_kernel, half_cap),
        out_shape=jax.ShapeDtypeStruct(hidden.shape, BF16),
        in_specs=[pl.BlockSpec(memory_space=pltpu.VMEM)] * 4,
        out_specs=pl.BlockSpec(memory_space=pltpu.VMEM),
        cost_estimate=pl.CostEstimate(
            flops=8 * returned.size * hidden.shape[1], bytes_accessed=2 * returned.size, transcendentals=0
        ),
    )(returned, hidden, slots, weights)


def ring_pairs(shards):
    pairs = []
    for source in range(shards):
        line, place, core = source // (2 * RING), source // 2 % RING, source % 2
        step = 1 if place % 2 == core else RING - 1
        pairs.append((source, (line * RING + (place + step) % RING) * 2 + core))
    return pairs


def slot_index(route_rows, n_experts, capacity):
    flat_ids = route_rows.reshape(-1)
    count = flat_ids.shape[0]
    onehot = flat_ids[:, None] == jnp.arange(n_experts, dtype=jnp.int32)[None, :]
    order = jnp.arange(count, dtype=jnp.int32)
    earlier = (order[:, None] > order[None, :]).astype(BF16)
    before = jnp.dot(earlier, onehot.astype(BF16), preferred_element_type=F32)
    position = jnp.sum(jnp.where(onehot, before, 0.0), axis=1).astype(jnp.int32)
    return (flat_ids * capacity + position).reshape(route_rows.shape)


def local(
    resid, context, o_weight, gain, expert_ids, combine_codes, gate_weight, up_weight, down_weight
):
    n_experts = lax.axis_size("branch")
    n_groups = lax.axis_size("group")
    shards = n_groups * MEMBERS
    tok_rows, feat_width = resid.shape
    full_width = context.shape[1]
    capacity = 5 * tok_rows // (2 * n_experts)
    half_cap = capacity // 2
    quarter = n_experts // MEMBERS * half_cap
    half = -(-quarter // 16) * 16

    blocks = down_weight[0].reshape(-1, full_width // LANES, LANES).transpose(1, 0, 2).reshape(full_width, LANES)
    own = jnp.stack([gate_weight[0], up_weight[0], blocks])
    beside = lax.ppermute(own, SHARD, ring_pairs(shards))
    own_core = lax.ppermute(own, "core", [(0, 1), (1, 0)])

    piece = -(-(full_width * feat_width) // (LANES * ROWS * n_experts)) * ROWS
    tiles = cut(o_weight[0].T, n_experts * piece).reshape(n_experts, piece, LANES)
    parts = lax.all_to_all(tiles, "branch", 0, 0, tiled=True)
    mean_part = (jnp.sum(parts.astype(F32), axis=0) / n_experts).astype(BF16)
    spread = jnp.broadcast_to(mean_part[None], (n_experts, piece, LANES))
    all_parts = lax.all_to_all(spread, "branch", 0, 0, tiled=True).reshape(n_experts * piece, LANES)

    slots = slot_index(expert_ids, n_experts, capacity)
    merged, hidden, sent = hidden_rows(all_parts, context, resid.T, slots.T, n_experts, half_cap)
    hidden, beside = lax.optimization_barrier((hidden, beside))
    beside_core = lax.ppermute(beside, "core", [(0, 1), (1, 0)])
    arrived = lax.all_to_all(sent.reshape(n_experts, SLOT_ROWS, LANES), "branch", 0, 0, tiled=True)
    arrived = arrived[:, :half_cap]

    quarters = jnp.pad(arrived.reshape(MEMBERS, quarter, LANES), ((0, 0), (0, half - quarter), (0, 0)))
    copies = jnp.broadcast_to(quarters[None], (n_groups, MEMBERS, half, LANES)).reshape(shards, half, LANES)
    gathered = lax.all_to_all(copies, SHARD, 0, 0, tiled=True)
    partial_out = run_expert(gathered, gain.astype(F32).reshape(1, -1), (own, own_core, beside, beside_core))
    exchanged = lax.all_to_all(partial_out, SHARD, 0, 0, tiled=True)
    expert_out = jnp.sum(exchanged.reshape(n_groups, MEMBERS, half, LANES).astype(F32), axis=0).astype(BF16)

    expert_out = expert_out[:, :quarter].reshape(n_experts, half_cap, LANES)
    expert_out = jnp.pad(expert_out, ((0, 0), (0, SLOT_ROWS - half_cap), (0, 0)))
    returned = lax.all_to_all(expert_out, "branch", 0, 0, tiled=True).reshape(n_experts * SLOT_ROWS, LANES)
    code_vals = combine_codes.astype(F32)
    mix_weights = code_vals / jnp.sum(code_vals, axis=1, keepdims=True)
    mixed = combine(returned, hidden, slots.T, mix_weights.T, half_cap)
    return (mixed.T, merged.T)


def solution(mesh):
    n_branches, n_shards = mesh.devices.shape
    fine = Mesh(mesh.devices.reshape(n_branches, n_shards // MEMBERS, 2, 2), ("branch",) + SHARD)
    in_specs = (
        P("branch", SHARD),
        P("branch", None),
        P("branch", None, SHARD),
        P(),
        P("branch", None),
        P("branch", None),
        P("branch", None, SHARD),
        P("branch", None, SHARD),
        P("branch", SHARD, None),
    )
    out_specs = (P("branch", SHARD), P(None, SHARD))
    return jax.shard_map(local, mesh=fine, in_specs=in_specs, out_specs=out_specs, check_vma=False)
```

```python
import functools

import jax
import jax.numpy as jnp
from jax import lax
from jax.experimental import pallas as pl
from jax.experimental.pallas import tpu as pltpu
from jax.sharding import Mesh, PartitionSpec as P

epsilon = 1e-05
MEMBERS = 4
OUT_PARTS = 4
ROWS = 16
SLOT_ROWS = 32
RING = 8
SHARD = ("group", "chip", "core")
LANES = 128
BF16 = jnp.bfloat16
F32 = jnp.float32


def expert_kernel(x_ref, gain_ref, *refs):
    given, (out_any, out_ref, rows_ref, weights, sems, out_sems) = refs[:MEMBERS], refs[MEMBERS:]

    def fetch(m, kind):
        return pltpu.make_async_copy(given[m].at[kind], weights.at[m, kind], sems.at[m, kind])

    for m in range(MEMBERS):
        fetch(m, 0).start()
        fetch(m, 1).start()
    sources, half, _ = x_ref.shape
    width = rows_ref.shape[1]
    low = lax.broadcasted_iota(jnp.int32, (half, LANES), 1) < LANES // 2
    squares = [jnp.zeros((half, LANES), F32), jnp.zeros((half, LANES), F32)]
    for q in range(sources // 2):
        even, odd = x_ref[2 * q].astype(F32), x_ref[2 * q + 1].astype(F32)
        top = jnp.where(low, even, pltpu.roll(odd, LANES // 2, 1))
        bottom = jnp.where(low, pltpu.roll(even, LANES // 2, 1), odd)
        squares[0] += top * top
        squares[1] += bottom * bottom
        rows_ref[:half, q * LANES : (q + 1) * LANES] = top.astype(BF16)
        rows_ref[half:, q * LANES : (q + 1) * LANES] = bottom.astype(BF16)
    for m in range(MEMBERS):
        fetch(m, 2).start()
    total = jnp.sum(jnp.concatenate(squares, axis=0), axis=1, keepdims=True)
    inverse = lax.rsqrt(total / width + epsilon)
    chunk = 2 * LANES
    for k in range(0, width, chunk):
        gain = gain_ref[:, k : k + chunk]
        rows_ref[:, k : k + chunk] = (rows_ref[:, k : k + chunk].astype(F32) * inverse * gain).astype(BF16)
    inner = []
    for m in range(MEMBERS):
        fetch(m, 0).wait()
        fetch(m, 1).wait()
        acts = jnp.zeros((2 * half, 2 * LANES), F32)
        for k in range(0, width, chunk):
            both = jnp.concatenate([weights[m, 0, k : k + chunk, :], weights[m, 1, k : k + chunk, :]], axis=1)
            acts += jnp.dot(rows_ref[:, k : k + chunk], both, preferred_element_type=F32)
        gate_acts, up_acts = acts[:, :LANES], acts[:, LANES:]
        inner.append((gate_acts / (1.0 + jnp.exp(-gate_acts)) * up_acts).astype(BF16))
    inner = jnp.concatenate(inner, axis=1)
    for m in range(MEMBERS):
        fetch(m, 2).wait()
    leaving = []
    span = sources // OUT_PARTS
    for q in range(0, width // LANES, 2):
        columns = [
            jnp.concatenate([weights[m, 2, (q + j) * LANES : (q + j + 1) * LANES, :] for m in range(MEMBERS)], axis=0)
            for j in range(2)
        ]
        part = jnp.dot(inner, jnp.concatenate(columns, axis=1), preferred_element_type=F32)
        for j in range(2):
            s = 2 * (q + j)
            top = part[:half, j * LANES : (j + 1) * LANES]
            bottom = part[half:, j * LANES : (j + 1) * LANES]
            out_ref[s] = jnp.where(low, top, pltpu.roll(bottom, LANES // 2, 1)).astype(BF16)
            out_ref[s + 1] = jnp.where(low, pltpu.roll(top, LANES // 2, 1), bottom).astype(BF16)
        if (2 * q + 4) % span == 0:
            part = len(leaving)
            block = pl.ds(part * span, span)
            leaving.append(pltpu.make_async_copy(out_ref.at[block], out_any.at[block], out_sems.at[part]))
            leaving[-1].start()
    for copy in leaving:
        copy.wait()


def run_expert(x, gain, weights):
    sources, half, _ = x.shape
    width = gain.shape[1]
    size = sum(w.size for w in weights)
    return pl.pallas_call(
        expert_kernel,
        out_shape=jax.ShapeDtypeStruct(x.shape, BF16),
        in_specs=[pl.BlockSpec(memory_space=pltpu.VMEM)] * 2 + [pl.BlockSpec(memory_space=pl.ANY)] * MEMBERS,
        out_specs=pl.BlockSpec(memory_space=pl.ANY),
        scratch_shapes=[
            pltpu.VMEM(x.shape, BF16),
            pltpu.VMEM((2 * half, width), BF16),
            pltpu.VMEM((MEMBERS,) + weights[0].shape, BF16),
            pltpu.SemaphoreType.DMA((MEMBERS, 3)),
            pltpu.SemaphoreType.DMA((OUT_PARTS,)),
        ],
        compiler_params=pltpu.CompilerParams(vmem_limit_bytes=56 * 1024 * 1024),
        cost_estimate=pl.CostEstimate(
            flops=2 * 2 * half * size, bytes_accessed=2 * (2 * x.size + size), transcendentals=0
        ),
    )(x, gain, *weights)


def tile_of(number, width):
    across = width // LANES
    row, column = number // across * ROWS, number % across * LANES
    return slice(row, row + ROWS), slice(column, column + LANES)


def cut_kernel(columns_ref, out_ref):
    feats, width = columns_ref.shape
    tiles = feats // ROWS * (width // LANES)
    for t in range(tiles):
        rows, lanes = tile_of(t, width)
        out_ref[t * ROWS : (t + 1) * ROWS, :] = columns_ref[rows, lanes]
    if tiles * ROWS < out_ref.shape[0]:
        out_ref[tiles * ROWS :, :] = jnp.zeros((out_ref.shape[0] - tiles * ROWS, LANES), BF16)


def cut(columns, out_rows):
    return pl.pallas_call(
        cut_kernel,
        out_shape=jax.ShapeDtypeStruct((out_rows, LANES), BF16),
        in_specs=[pl.BlockSpec(memory_space=pltpu.VMEM)],
        out_specs=pl.BlockSpec(memory_space=pltpu.VMEM),
        cost_estimate=pl.CostEstimate(flops=0, bytes_accessed=4 * columns.size, transcendentals=0),
    )(columns)


def hidden_kernel(half_cap, parts_ref, context_ref, resid_ref, slots_ref, merged_ref, hidden_ref, sent_ref):
    feats, width = merged_ref.shape
    tokens = context_ref.shape[0]
    for t in range(feats // ROWS * (width // LANES)):
        rows, lanes = tile_of(t, width)
        merged_ref[rows, lanes] = parts_ref[t * ROWS : (t + 1) * ROWS, :]
    across = (((1,), (1,)), ((), ()))
    product = lax.dot_general(merged_ref[...], context_ref[...], across, preferred_element_type=F32)
    hidden = (resid_ref[...].astype(F32) + product).astype(BF16)
    hidden_ref[...] = hidden
    count = sent_ref.shape[0]
    row = lax.broadcasted_iota(jnp.int32, (count, tokens), 0)
    place, expert = row % SLOT_ROWS, row // SLOT_ROWS
    empty = jnp.zeros((LANES - feats, tokens), BF16)
    sent = jnp.zeros((count, LANES), F32)
    for side in range(2):
        slot = jnp.where(place < half_cap, (2 * expert + side) * half_cap + place, -1)
        table = ((slots_ref[0:1, :] == slot) | (slots_ref[1:2, :] == slot)).astype(F32).astype(BF16)
        lanes = jnp.concatenate([hidden, empty] if side == 0 else [empty, hidden], axis=0)
        sent += lax.dot_general(table, lanes, across, preferred_element_type=F32)
    sent_ref[...] = sent.astype(BF16)


def hidden_rows(parts, context, resid, slots, n_experts, half_cap):
    feats, tokens = resid.shape
    width = context.shape[1]
    return pl.pallas_call(
        functools.partial(hidden_kernel, half_cap),
        out_shape=(
            jax.ShapeDtypeStruct((feats, width), BF16),
            jax.ShapeDtypeStruct((feats, tokens), BF16),
            jax.ShapeDtypeStruct((n_experts * SLOT_ROWS, LANES), BF16),
        ),
        in_specs=[pl.BlockSpec(memory_space=pltpu.VMEM)] * 4,
        out_specs=[pl.BlockSpec(memory_space=pltpu.VMEM)] * 3,
        cost_estimate=pl.CostEstimate(
            flops=2 * feats * tokens * width, bytes_accessed=2 * (2 * feats + tokens) * width, transcendentals=0
        ),
    )(parts, context, resid, slots)


def ring_pairs(shards):
    pairs = []
    for source in range(shards):
        line, place, core = source // (2 * RING), source // 2 % RING, source % 2
        step = 1 if place % 2 == core else RING - 1
        pairs.append((source, (line * RING + (place + step) % RING) * 2 + core))
    return pairs


def slot_index(route_rows, n_experts, capacity):
    flat_ids = route_rows.reshape(-1)
    count = flat_ids.shape[0]
    onehot = flat_ids[:, None] == jnp.arange(n_experts, dtype=jnp.int32)[None, :]
    order = jnp.arange(count, dtype=jnp.int32)
    earlier = (order[:, None] > order[None, :]).astype(BF16)
    before = jnp.dot(earlier, onehot.astype(BF16), preferred_element_type=F32)
    position = jnp.sum(jnp.where(onehot, before, 0.0), axis=1).astype(jnp.int32)
    return (flat_ids * capacity + position).reshape(route_rows.shape)


def local(
    resid, context, o_weight, gain, expert_ids, combine_codes, gate_weight, up_weight, down_weight
):
    n_experts = lax.axis_size("branch")
    n_groups = lax.axis_size("group")
    shards = n_groups * MEMBERS
    tok_rows, feat_width = resid.shape
    full_width = context.shape[1]
    capacity = 5 * tok_rows // (2 * n_experts)
    half_cap = capacity // 2
    quarter = n_experts // MEMBERS * half_cap
    half = -(-quarter // 16) * 16

    blocks = down_weight[0].reshape(-1, full_width // LANES, LANES).transpose(1, 0, 2).reshape(full_width, LANES)
    own = jnp.stack([gate_weight[0], up_weight[0], blocks])
    beside = lax.ppermute(own, SHARD, ring_pairs(shards))
    own_core = lax.ppermute(own, "core", [(0, 1), (1, 0)])

    piece = -(-(full_width * feat_width) // (LANES * ROWS * n_experts)) * ROWS
    tiles = cut(o_weight[0].T, n_experts * piece).reshape(n_experts, piece, LANES)
    parts = lax.all_to_all(tiles, "branch", 0, 0, tiled=True)
    mean_part = (jnp.sum(parts.astype(F32), axis=0) / n_experts).astype(BF16)
    spread = jnp.broadcast_to(mean_part[None], (n_experts, piece, LANES))
    all_parts = lax.all_to_all(spread, "branch", 0, 0, tiled=True).reshape(n_experts * piece, LANES)

    slots = slot_index(expert_ids, n_experts, capacity)
    merged, hidden, sent = hidden_rows(all_parts, context, resid.T, slots.T, n_experts, half_cap)
    merged, hidden_state = merged.T, hidden.T
    hidden_state, beside = lax.optimization_barrier((hidden_state, beside))
    beside_core = lax.ppermute(beside, "core", [(0, 1), (1, 0)])
    arrived = lax.all_to_all(sent.reshape(n_experts, SLOT_ROWS, LANES), "branch", 0, 0, tiled=True)
    arrived = arrived[:, :half_cap]

    quarters = jnp.pad(arrived.reshape(MEMBERS, quarter, LANES), ((0, 0), (0, half - quarter), (0, 0)))
    copies = jnp.broadcast_to(quarters[None], (n_groups, MEMBERS, half, LANES)).reshape(shards, half, LANES)
    gathered = lax.all_to_all(copies, SHARD, 0, 0, tiled=True)
    partial_out = run_expert(gathered, gain.astype(F32).reshape(1, -1), (own, own_core, beside, beside_core))
    exchanged = lax.all_to_all(partial_out, SHARD, 0, 0, tiled=True)
    expert_out = jnp.sum(exchanged.reshape(n_groups, MEMBERS, half, LANES).astype(F32), axis=0).astype(BF16)

    expert_out = expert_out[:, :quarter].reshape(n_experts, half_cap, LANES)
    returned = lax.all_to_all(expert_out, "branch", 0, 0, tiled=True)
    returned = jnp.stack([returned[:, :, :feat_width], returned[:, :, feat_width:]], axis=1)
    returned = returned.reshape(n_experts * capacity, feat_width)
    all_slots = jnp.arange(n_experts * capacity, dtype=jnp.int32)
    code_vals = combine_codes.astype(F32)
    mix_weights = code_vals / jnp.sum(code_vals, axis=1, keepdims=True)
    mixture = jnp.zeros((tok_rows, feat_width), F32)
    for k in range(2):
        table = (slots[:, k, None] == all_slots[None, :]).astype(BF16)
        picked = jnp.dot(table, returned, preferred_element_type=F32)
        mixture += picked * mix_weights[:, k, None]
    mixed = (hidden_state.astype(F32) + mixture).astype(BF16)
    return (mixed, merged)


def solution(mesh):
    n_branches, n_shards = mesh.devices.shape
    fine = Mesh(mesh.devices.reshape(n_branches, n_shards // MEMBERS, 2, 2), ("branch",) + SHARD)
    in_specs = (
        P("branch", SHARD),
        P("branch", None),
        P("branch", None, SHARD),
        P(),
        P("branch", None),
        P("branch", None),
        P("branch", None, SHARD),
        P("branch", None, SHARD),
        P("branch", SHARD, None),
    )
    out_specs = (P("branch", SHARD), P(None, SHARD))
    return jax.shard_map(local, mesh=fine, in_specs=in_specs, out_specs=out_specs, check_vma=False)
```
